32 devices in a mesh: parts: 2 (over x), leaf: 16 (over z, y, core).
Axes of the slice: x: 2, y: 2, z: 4, core: 2. Of those that a mesh axis runs over, the one named last changes fastest.
Arguments:
- features: bfloat16 [65536, 256], P(('parts', 'leaf')), parts along dimension 0, may hold values from -4 to 4
- rhs: bfloat16 [65536], P(('parts', 'leaf')), parts along dimension 0, may hold values from -6 to 6
- leaf_order: int32 [65536], P(('parts', 'leaf')), parts along dimension 0, may hold values from 0 to 2047, as said below
- leaf_inverse: bfloat16 [65536, 2048], P(('parts', 'leaf')), parts along dimension 0, may hold values from -2 to 2.5, as said below
- landmarks: bfloat16 [14, 256, 256], P('parts'), parts along dimension 0, may hold values from -4 to 4
- core_factor: float32 [14, 256, 256], P('parts'), parts along dimension 0, may hold values from -1 to 1
Outputs:
- alpha: float32 [65536], P(('parts', 'leaf')), parts along dimension 0
- solved_basis: float32 [65536, 256], P(('parts', 'leaf')), parts along dimension 0
The draws below stay inside these ranges and needn't reach their ends.
There are 2 independent parts, one for each index of `parts`. The reference program is written for one: setup_inputs(seed, part) draws one part's arguments, and reference() takes and returns one part's arrays. A program takes and returns all parts, laid end to end along the dimension named above; each array names one. Nothing has to cross between parts.
Inputs may be any that keep to these rules, and one draw needn't show every extreme that they name: `leaf_order`: each aligned block of 2048 entries holds every number 0 to 2047 once. `leaf_inverse`: each leaf's block is symmetric positive definite.
All inputs are finite; a program needn't handle non-finite values.
Results may differ from the reference program's by a relative error of at most 0.012.
The reference program's roundings to bfloat16 on the way count: a program that leaves them out, or rounds other values in their place, can miss the bound.
Values sent between devices are 32-bit elements; how exact they have to be, the bound alone decides.
A program may use at most 128 MiB of HBM per device.

```python
import math
import jax
import jax.numpy as jnp
from jax import lax

F = 256
R = 256
ROWS = 2048
LEAVES = 16
N_ROWS = 32768


centre_width = 0.52


noise_width = 0.11


def spread_values(key, shape, width):
    return jax.random.truncated_normal(key, -4.0, 4.0, shape, jnp.float32) * width


def cluster_centres(key):
    per_leaf = max(1, R // LEAVES)
    return spread_values(jax.random.fold_in(key, 101), (LEAVES * per_leaf, F), centre_width)


def draw_features(key, part):
    centres = cluster_centres(key)
    key = jax.random.fold_in(key, 1)
    per_leaf = max(1, R // LEAVES)
    position = jnp.arange(N_ROWS, dtype=jnp.int32)
    cluster = position // ROWS * per_leaf + position % per_leaf
    noise = spread_values(key, (N_ROWS, F), noise_width)
    return (jnp.take(centres, cluster, axis=0) + noise).astype(jnp.bfloat16)


def draw_landmarks(key, part):
    centres = cluster_centres(key)
    key = jax.random.fold_in(key, 2)
    per_leaf = max(1, R // LEAVES)
    column = jnp.arange(R, dtype=jnp.int32)
    chosen = []
    for depth in range(3):
        leaves_node = LEAVES // 2 ** depth
        clusters_node = per_leaf * leaves_node
        for place in range(2 ** depth):
            first = place * leaves_node * per_leaf
            chosen.append(first + column * clusters_node // R)
    cluster = jnp.concatenate(chosen)
    noise = spread_values(key, (7 * R, F), noise_width)
    marks = jnp.take(centres, cluster, axis=0) + noise
    return marks.reshape(7, R, F).astype(jnp.bfloat16)


def draw_leaf_order(key, part):
    key = jax.random.fold_in(key, 3)
    keys = jax.random.split(key, LEAVES)
    orders = jax.vmap(lambda k: jax.random.permutation(k, ROWS))(keys)
    return orders.reshape(N_ROWS).astype(jnp.int32)


def draw_leaf_inverse(key, part):
    key = jax.random.fold_in(key, 4)
    first, second = jax.random.split(key)
    raw = jax.random.uniform(first, (LEAVES, ROWS, ROWS), jnp.float32, -1.0, 1.0)
    symmetric = 0.5 * (raw + jnp.swapaxes(raw, 1, 2))
    index = jnp.arange(ROWS)
    same = index[:, None] == index[None, :]
    off_part = jnp.where(same[None], 0.0, symmetric) * (1.2 / math.sqrt(ROWS))
    diagonal = jax.random.uniform(second, (LEAVES, ROWS), jnp.float32, 1.5, 2.5)
    blocks = off_part + jnp.where(same[None], diagonal[:, :, None], 0.0)
    return blocks.reshape(N_ROWS, ROWS).astype(jnp.bfloat16)


def draw_core_factor(key, part):
    key = jax.random.fold_in(key, 5)
    per_leaf = max(1, R // LEAVES)
    depths = [0, 1, 1, 2, 2, 2, 2]
    values = [0.85 * per_leaf * math.sqrt(LEAVES / 2.0 ** d) / (R * math.sqrt(ROWS)) for d in depths]
    scales = jnp.array(values, dtype=jnp.float32)
    return spread_values(key, (7, R, R), 1.0) * scales[:, None, None]


def level_of(stream_key, shape, cuts, low, top_value):
    loudness = 1.0
    for dim, blocks in cuts:
        draws = jax.random.uniform(jax.random.fold_in(jax.random.fold_in(stream_key, 6), dim), (blocks,), jnp.float32, low / len(cuts), top_value / len(cuts))
        loudness = loudness * jnp.repeat(jnp.exp(draws), shape[dim] // blocks).reshape((-1,) + (1,) * (len(shape) - 1 - dim))
    return loudness


def bell_draw(key, extent, spread, bound, cuts=(), kind=jnp.bfloat16):
    values = spread * jax.random.normal(key, extent, jnp.float32)
    if cuts:
        values = values * level_of(key, extent, cuts, -0.22, 0.18)
    return jnp.clip(values, -bound, bound).astype(kind)


def setup_inputs(seed: int = 0, part: int = 0) -> dict:
    key_of = jax.random.split(jax.random.key(seed), 7)
    part_keys = jax.random.split(jax.random.fold_in(key_of[6], part), 7)
    features = draw_features(jax.random.fold_in(jax.random.fold_in(key_of[6], part), 71), part)
    rhs = bell_draw(part_keys[1], (N_ROWS,), 1.0, 6.0, ((0, 16),))
    leaf_order = draw_leaf_order(jax.random.fold_in(jax.random.fold_in(key_of[6], part), 71), part)
    leaf_inverse = draw_leaf_inverse(jax.random.fold_in(jax.random.fold_in(key_of[6], part), 71), part)
    landmarks = draw_landmarks(jax.random.fold_in(jax.random.fold_in(key_of[6], part), 71), part)
    core_factor = draw_core_factor(jax.random.fold_in(jax.random.fold_in(key_of[6], part), 71), part)
    return dict(features=features, rhs=rhs, leaf_order=leaf_order, leaf_inverse=leaf_inverse, landmarks=landmarks, core_factor=core_factor)


length_scale = 5.0
root_five = math.sqrt(5.0)
highest = lax.Precision.HIGHEST

def matern(rows, marks):
    cross = lax.dot_general(rows.astype(jnp.float32), marks.astype(jnp.float32), (((1,), (1,)), ((), ())), preferred_element_type=jnp.float32)
    row_sq = lax.optimization_barrier(jnp.sum(jnp.square(rows.astype(jnp.float32)), axis=1))
    mark_sq = lax.optimization_barrier(jnp.sum(jnp.square(marks.astype(jnp.float32)), axis=1))
    dist_sq = row_sq[:, None] + mark_sq[None, :] - 2.0 * cross
    scaled = root_five * jnp.sqrt(dist_sq + 1e-06) / length_scale
    return ((1.0 + scaled + scaled * scaled / 3.0) * jnp.exp(-scaled)).astype(jnp.bfloat16)

def reference(features, rhs, leaf_order, leaf_inverse, landmarks, core_factor):
    digits = LEAVES.bit_length() - 1
    feats = features.reshape(LEAVES, ROWS, F)
    order = leaf_order.reshape(LEAVES, ROWS)
    tree_x = jnp.take_along_axis(feats, order[:, :, None], axis=1)
    tree_y = jnp.take_along_axis(rhs.reshape(LEAVES, ROWS), order, axis=1)
    inverse = leaf_inverse.reshape(LEAVES, ROWS, ROWS)

    def leaf_block(items):
        rows, scores, block, leaf = items
        bases = []
        for level in range(3):
            node = 2 ** level - 1 + leaf // 2 ** (digits - level)
            marks = lax.dynamic_index_in_dim(landmarks, node, 0, keepdims=False)
            bases.append(matern(rows, marks))
        solved = jnp.stack([jnp.dot(block.astype(jnp.float32), b.astype(jnp.float32), preferred_element_type=jnp.float32) for b in bases])
        first = jnp.dot(block.astype(jnp.float32), scores.astype(jnp.float32), preferred_element_type=jnp.float32)
        return (jnp.stack(bases), solved, first)
    basis, solved, vector = lax.map(leaf_block, (tree_x, tree_y, inverse, jnp.arange(LEAVES, dtype=jnp.int32)))
    sets = [solved[:, q] for q in range(3)]
    eye = jnp.eye(R, dtype=jnp.float32)
    for level in (2, 1, 0):
        count = 2 ** level
        span = LEAVES // count * ROWS
        basis_now = basis[:, level].astype(jnp.float32).reshape(count, span, R)
        targets = [sets[q].reshape(count, span, R) for q in range(level + 1)]
        own = targets[level]
        vec = vector.reshape(count, span)
        projections = [jnp.einsum('cnk,cnj->ckj', basis_now, t, precision=highest) for t in targets]
        proj_vec = jnp.einsum('cnk,cn->ck', basis_now, vec, precision=highest)
        factor = core_factor[count - 1:2 * count - 1]
        factor_t = jnp.swapaxes(factor, 1, 2)
        capacity = eye + jnp.matmul(factor_t, jnp.matmul(projections[level], factor, precision=highest), precision=highest)
        lower = jnp.linalg.cholesky(capacity)
        middle = jax.vmap(lambda c, b: jax.scipy.linalg.cho_solve((c, True), b))(lower, factor_t)
        mixer = jnp.matmul(factor, middle, precision=highest)
        new_sets = []
        for q in range(level + 1):
            change = jnp.matmul(mixer, projections[q], precision=highest)
            new_sets.append((targets[q] - jnp.einsum('cnk,ckj->cnj', own, change, precision=highest)).reshape(LEAVES, ROWS, R))
        change_vec = jnp.einsum('ckj,cj->ck', mixer, proj_vec, precision=highest)
        vector = (vec - jnp.einsum('cnk,ck->cn', own, change_vec, precision=highest)).reshape(LEAVES, ROWS)
        sets = new_sets + sets[level + 1:]
    return (vector.reshape(N_ROWS), sets[0].reshape(N_ROWS, R))
```

```python
import functools
import math

import jax
import jax.numpy as jnp
from jax import lax
from jax.experimental import pallas as pl
from jax.experimental.pallas import tpu as pltpu
from jax.sharding import PartitionSpec as P

length_scale = 5.0
root_five = math.sqrt(5.0)
highest = lax.Precision.HIGHEST
MESH = pl.DeviceIdType.MESH
BLOCK = 32
VEC = 8


def matern(rows, marks):
    cross = lax.dot_general(
        rows, marks, (((1,), (1,)), ((), ())), preferred_element_type=jnp.float32
    )
    row_sq = jnp.sum(jnp.square(rows.astype(jnp.float32)), axis=1)
    mark_sq = jnp.sum(jnp.square(marks.astype(jnp.float32)), axis=1)
    dist_sq = row_sq[:, None] + mark_sq[None, :] - 2.0 * cross
    scaled = root_five * jnp.sqrt(dist_sq + 1e-06) / length_scale
    return ((1.0 + scaled + scaled * scaled / 3.0) * jnp.exp(-scaled)).astype(jnp.bfloat16)


def halves(x):
    high = x.astype(jnp.bfloat16)
    low = (x - high.astype(jnp.float32)).astype(jnp.bfloat16)
    return high, low


def dot32(a, b, dims):
    return lax.dot_general(
        a, b, (dims, ((), ())), precision=highest, preferred_element_type=jnp.float32
    )


NN = ((1,), (0,))
TN = ((0,), (0,))
NT = ((1,), (1,))


def sum_kernel(bits, differ, x_ref, out_ref, acc, got, send_sem, recv_sem):
    leaf = lax.axis_index("leaf")
    core = lax.rem(leaf, 2)
    half = x_ref.shape[0] // 2
    mine = pl.ds(pl.multiple_of(core * half, 8), half)
    other = pl.ds(pl.multiple_of((1 - core) * half, 8), half)
    sibling = leaf + 1 - 2 * core
    partners = []
    for bit in bits:
        on = lax.rem(leaf // (1 << bit), 2)
        partners.append(leaf + (1 - 2 * on) * (1 << bit))
    barrier = pltpu.get_barrier_semaphore()
    for device in [sibling] + partners:
        pl.semaphore_signal(barrier, inc=1, device_id={"leaf": device}, device_id_type=MESH)
    pl.semaphore_wait(barrier, 1 + len(partners))

    def send(src, dst, slot, device):
        copy = pltpu.make_async_remote_copy(
            src_ref=src,
            dst_ref=dst,
            send_sem=send_sem.at[slot],
            recv_sem=recv_sem.at[slot],
            device_id={"leaf": device},
            device_id_type=MESH,
        )
        copy.start()
        return copy

    n = len(bits)
    if differ:
        copy = send(x_ref.at[other], got.at[n], n, sibling)
        copy.wait()
        acc[0] = x_ref[mine] + got[n]
    else:
        acc[0] = x_ref[mine]
    for i, device in enumerate(partners):
        copy = send(acc.at[i], got.at[i], i, device)
        copy.wait()
        acc[i + 1] = acc[i] + got[i]
    out_ref[mine] = acc[n]
    copy = send(acc.at[n], out_ref.at[mine], n + 1, sibling)
    copy.wait()


def node_sum(x, bits, differ, number):
    n = len(bits)
    half = x.shape[0] // 2
    return pl.pallas_call(
        functools.partial(sum_kernel, bits, differ),
        out_shape=jax.ShapeDtypeStruct(x.shape, jnp.float32),
        in_specs=[pl.BlockSpec(memory_space=pltpu.VMEM)],
        out_specs=pl.BlockSpec(memory_space=pltpu.VMEM),
        scratch_shapes=[
            pltpu.VMEM((n + 1, half, x.shape[1]), jnp.float32),
            pltpu.VMEM((n + 1, half, x.shape[1]), jnp.float32),
            pltpu.SemaphoreType.DMA((n + 2,)),
            pltpu.SemaphoreType.DMA((n + 2,)),
        ],
        compiler_params=pltpu.CompilerParams(
            collective_id=number, has_side_effects=True, vmem_limit_bytes=32 << 20
        ),
        name="node_sum",
    )(x)


def invert_small(d):
    size = d.shape[0]
    sub = lax.broadcasted_iota(jnp.int32, d.shape, 0)
    lane = lax.broadcasted_iota(jnp.int32, d.shape, 1)
    for k in range(size):
        column = jnp.broadcast_to(d[:, k : k + 1], d.shape)
        scale = 1.0 / column[k : k + 1, :]
        row = jnp.where(lane[:1] == k, -1.0, d[k : k + 1, :]) * scale
        column = jnp.where(sub == k, -1.0, column)
        d = jnp.where((sub == k) | (lane == k), 0.0, d) - column * row
    return -d


def invert(a_ref):
    size = a_ref.shape[0]
    sub = lax.broadcasted_iota(jnp.int32, (size, size), 0) // BLOCK
    lane = lax.broadcasted_iota(jnp.int32, (size, size), 1) // BLOCK
    eye_row = lax.broadcasted_iota(jnp.int32, (BLOCK, size), 0)
    eye_lane = lax.broadcasted_iota(jnp.int32, (BLOCK, size), 1)
    for k in range(size // BLOCK):
        first = k * BLOCK
        rows = a_ref[first : first + BLOCK, :]
        small = invert_small(rows[:, first : first + BLOCK])
        minus = jnp.where(eye_row + first == eye_lane, -1.0, 0.0)
        panel = jnp.where(eye_lane // BLOCK == k, minus, rows)
        scaled = dot32(small, panel, NN)
        rest = jnp.where((sub == k) | (lane == k), 0.0, a_ref[...])
        a_ref[...] = rest - dot32(panel, scaled, TN)


def mix(gram, factor, a_ref):
    size = factor.shape[0]
    same = lax.broadcasted_iota(jnp.int32, (size, size), 0) == lax.broadcasted_iota(
        jnp.int32, (size, size), 1
    )
    a_ref[...] = jnp.where(same, 1.0, 0.0) + dot32(factor, dot32(gram, factor, NN), TN)
    invert(a_ref)
    return dot32(factor, dot32(-a_ref[...], factor, NT), NN)


def level_two(s_ref, f_ref, next_ref, x_ref, xv_ref, a_ref):
    w = f_ref.shape[0]
    mixer = mix(s_ref[2 * w : 3 * w], f_ref[...], a_ref)
    t20, t21 = s_ref[0:w], s_ref[w : 2 * w]
    x20, x21 = dot32(mixer, t20, NN), dot32(mixer, t21, NN)
    x_ref[0:w] = x20
    x_ref[w : 2 * w] = x21
    vecs = 6 * w
    h0, h1, h2 = [s_ref[vecs + i * VEC : vecs + (i + 1) * VEC] for i in range(3)]
    xv = dot32(h2, mixer, NN)
    xv_ref[...] = xv
    next_ref[0:w] = s_ref[3 * w : 4 * w] - dot32(t21, x20, TN)
    next_ref[w : 2 * w] = s_ref[4 * w : 5 * w] - dot32(t21, x21, TN)
    next_ref[2 * w : 3 * w] = s_ref[5 * w : 6 * w] - dot32(t20, x20, TN)
    next_ref[3 * w : 3 * w + VEC] = h0 - dot32(xv, t20, NN)
    next_ref[3 * w + VEC : 3 * w + 2 * VEC] = h1 - dot32(xv, t21, NN)


def level_one(s_ref, f_ref, x2_ref, x2v_ref, next_ref, x_ref, xv_ref, a_ref):
    w = f_ref.shape[0]
    mixer = mix(s_ref[w : 2 * w], f_ref[...], a_ref)
    t10 = s_ref[0:w]
    x10 = dot32(mixer, t10, NN)
    h0, h1 = [s_ref[3 * w + i * VEC : 3 * w + (i + 1) * VEC] for i in range(2)]
    xv = dot32(h1, mixer, NN)
    next_ref[0:w] = s_ref[2 * w : 3 * w] - dot32(t10, x10, TN)
    next_ref[w : w + VEC] = h0 - dot32(xv, t10, NN)
    next_ref[w + VEC :] = jnp.zeros_like(next_ref[w + VEC :])
    x21 = x2_ref[w : 2 * w]
    x_ref[0:w] = x10
    x_ref[w : 2 * w] = x2_ref[0:w] - dot32(x21, x10, NN)
    xv_ref[0:VEC] = xv
    xv_ref[VEC : 2 * VEC] = x2v_ref[...] - dot32(xv, x21, NT)


def level_zero(s_ref, f_ref, x1_ref, x1v_ref, k_ref, kv_ref, a_ref):
    w = f_ref.shape[0]
    gram = s_ref[0:w]
    mixer = mix(gram, f_ref[...], a_ref)
    x00 = dot32(mixer, gram, NN)
    xv = dot32(s_ref[w : w + VEC], mixer, NN)
    k_ref[0:w] = x00
    kv_ref[0:VEC] = xv
    for i in range(2):
        x = x1_ref[i * w : (i + 1) * w]
        k_ref[(i + 1) * w : (i + 2) * w] = x - dot32(x, x00, NN)
        v = x1v_ref[i * VEC : (i + 1) * VEC]
        kv_ref[(i + 1) * VEC : (i + 2) * VEC] = v - dot32(xv, x, NT)


def level_call(body, name, args, outs):
    w = args[1].shape[0]
    return pl.pallas_call(
        body,
        out_shape=[jax.ShapeDtypeStruct((rows, w), jnp.float32) for rows in outs],
        in_specs=[pl.BlockSpec(memory_space=pltpu.VMEM)] * len(args),
        out_specs=[pl.BlockSpec(memory_space=pltpu.VMEM)] * len(outs),
        scratch_shapes=[pltpu.VMEM((w, w), jnp.float32)],
        compiler_params=pltpu.CompilerParams(vmem_limit_bytes=32 << 20),
        name=name,
    )(*args)


def per_device(features, rhs, leaf_order, leaf_inverse, landmarks, core_factor):
    leaf = lax.axis_index("leaf")
    digits = lax.axis_size("leaf").bit_length() - 1
    rows = features.shape[0]
    w = core_factor.shape[1]
    pick = (leaf_order[:, None] == jnp.arange(rows, dtype=jnp.int32)[None, :]).astype(jnp.bfloat16)
    tree_x = jnp.dot(pick, features, preferred_element_type=jnp.float32).astype(jnp.bfloat16)
    tree_y = jnp.dot(pick, rhs, preferred_element_type=jnp.float32).astype(jnp.bfloat16)
    bases, factors = [], []
    for level in range(3):
        node = 2**level - 1 + jnp.right_shift(leaf, digits - level)
        marks = lax.dynamic_index_in_dim(landmarks, node, 0, keepdims=False)
        bases.append(matern(tree_x, marks))
        factors.append(lax.dynamic_index_in_dim(core_factor, node, 0, keepdims=False))
    basis = jnp.concatenate(bases, axis=1)
    solved = jnp.dot(leaf_inverse, basis, preferred_element_type=jnp.float32)
    vector = jnp.dot(leaf_inverse, tree_y, preferred_element_type=jnp.float32)
    high, low = halves(solved)

    def block(q, l):
        return sum(
            lax.dot_general(
                bases[l], part[:, q * w : (q + 1) * w], (TN, ((), ())),
                preferred_element_type=jnp.float32,
            )
            for part in (high, low)
        )

    v_high, v_low = halves(vector)
    h = sum(jnp.dot(part[None, :], basis, preferred_element_type=jnp.float32) for part in (v_high, v_low))
    h = jnp.broadcast_to(h.reshape(3, 1, w), (3, VEC, w)).reshape(3 * VEC, w)
    buf = jnp.concatenate(
        [block(0, 2), block(1, 2), block(2, 2), block(0, 1), block(1, 1), block(0, 0), h,
         jnp.zeros((VEC, w), jnp.float32)],
        axis=0,
    )
    buf = node_sum(buf, tuple(range(1, digits - 2)), True, 0)
    buf, x2, x2v = level_call(
        level_two, "level_two", (buf, factors[2]), (3 * w + 2 * VEC, 2 * w, VEC)
    )
    buf = node_sum(buf, (digits - 2,), False, 1)
    buf, x1, x1v = level_call(
        level_one, "level_one", (buf, factors[1], x2, x2v), (w + 2 * VEC, 2 * w, 2 * VEC)
    )
    buf = node_sum(buf, (digits - 1,), False, 2)
    k, kv = level_call(level_zero, "level_zero", (buf, factors[0], x1, x1v), (3 * w, 3 * VEC))
    k_high, k_low = halves(k)
    change = (
        jnp.dot(high, k_high, preferred_element_type=jnp.float32)
        + jnp.dot(high, k_low, preferred_element_type=jnp.float32)
        + jnp.dot(low, k_high, preferred_element_type=jnp.float32)
    )
    kv = kv.reshape(3, VEC, w)[:, 0].reshape(3 * w)
    alpha = vector - jnp.sum(solved * kv[None, :], axis=1)
    return (alpha, solved[:, :w] - change)


def solution(mesh):
    in_specs = (
        P(("parts", "leaf"), None),
        P(("parts", "leaf")),
        P(("parts", "leaf")),
        P(("parts", "leaf"), None),
        P("parts", None, None),
        P("parts", None, None),
    )
    out_specs = (P(("parts", "leaf")), P(("parts", "leaf"), None))
    return jax.shard_map(
        per_device, mesh=mesh, in_specs=in_specs, out_specs=out_specs, check_vma=False
    )
```

```python
import functools
import math

import jax
import jax.numpy as jnp
from jax import lax
from jax.experimental import pallas as pl
from jax.experimental.pallas import tpu as pltpu
from jax.sharding import PartitionSpec as P

length_scale = 5.0
root_five = math.sqrt(5.0)
highest = lax.Precision.HIGHEST
MESH = pl.DeviceIdType.MESH
BLOCK = 32
GROUP = 16
TILE = 256
PAD = 128
VEC = 8


def halves(x):
    high = x.astype(jnp.bfloat16)
    low = (x - high.astype(jnp.float32)).astype(jnp.bfloat16)
    return high, low


def dot32(a, b, dims):
    return lax.dot_general(
        a, b, (dims, ((), ())), precision=highest, preferred_element_type=jnp.float32
    )


NN = ((1,), (0,))
TN = ((0,), (0,))
NT = ((1,), (1,))


def sum_kernel(bits, differ, x_ref, out_ref, acc, got, send_sem, recv_sem):
    leaf = lax.axis_index("leaf")
    core = lax.rem(leaf, 2)
    half = x_ref.shape[0] // 2
    mine = pl.ds(pl.multiple_of(core * half, 8), half)
    other = pl.ds(pl.multiple_of((1 - core) * half, 8), half)
    sibling = leaf + 1 - 2 * core
    partners = []
    for bit in bits:
        on = lax.rem(leaf // (1 << bit), 2)
        partners.append(leaf + (1 - 2 * on) * (1 << bit))
    barrier = pltpu.get_barrier_semaphore()
    for device in [sibling] + partners:
        pl.semaphore_signal(barrier, inc=1, device_id={"leaf": device}, device_id_type=MESH)
    pl.semaphore_wait(barrier, 1 + len(partners))

    def send(src, dst, slot, device):
        copy = pltpu.make_async_remote_copy(
            src_ref=src,
            dst_ref=dst,
            send_sem=send_sem.at[slot],
            recv_sem=recv_sem.at[slot],
            device_id={"leaf": device},
            device_id_type=MESH,
        )
        copy.start()
        return copy

    n = len(bits)
    if differ:
        copy = send(x_ref.at[other], got.at[n], n, sibling)
        copy.wait()
        acc[0] = x_ref[mine] + got[n]
    else:
        acc[0] = x_ref[mine]
    for i, device in enumerate(partners):
        copy = send(acc.at[i], got.at[i], i, device)
        copy.wait()
        acc[i + 1] = acc[i] + got[i]
    out_ref[mine] = acc[n]
    copy = send(acc.at[n], out_ref.at[mine], n + 1, sibling)
    copy.wait()


def node_sum(x, bits, differ, number):
    n = len(bits)
    half = x.shape[0] // 2
    return pl.pallas_call(
        functools.partial(sum_kernel, bits, differ),
        out_shape=jax.ShapeDtypeStruct(x.shape, jnp.float32),
        in_specs=[pl.BlockSpec(memory_space=pltpu.VMEM)],
        out_specs=pl.BlockSpec(memory_space=pltpu.VMEM),
        scratch_shapes=[
            pltpu.VMEM((n + 1, half, x.shape[1]), jnp.float32),
            pltpu.VMEM((n + 1, half, x.shape[1]), jnp.float32),
            pltpu.SemaphoreType.DMA((n + 2,)),
            pltpu.SemaphoreType.DMA((n + 2,)),
        ],
        compiler_params=pltpu.CompilerParams(
            collective_id=number, has_side_effects=True, vmem_limit_bytes=32 << 20
        ),
        name="node_sum",
    )(x)


def sweep(rows, first):
    size = rows.shape[0]
    sub = lax.broadcasted_iota(jnp.int32, rows.shape, 0)
    lane = lax.broadcasted_iota(jnp.int32, rows.shape, 1)
    down = lax.broadcasted_iota(jnp.int32, (size, 128), 0)
    copies = rows.shape[1] // 128
    for start in range(0, size, GROUP):
        columns = []
        for i in range(GROUP):
            at = first + start + i
            columns.append(jnp.broadcast_to(rows[:, at : at + 1], (size, 128)))
        for i in range(GROUP):
            k = start + i
            scale = 1.0 / columns[i][k : k + 1, :]
            column = jnp.where(down == k, -1.0, columns[i])
            row = jnp.where(lane[:1] == first + k, -1.0, rows[k : k + 1, :])
            row = row * jnp.concatenate([scale] * copies, axis=1)
            for j in range(i + 1, GROUP):
                rest = jnp.where(down == k, 0.0, columns[j])
                columns[j] = rest - column * (columns[j][k : k + 1, :] * scale)
            rest = jnp.where((sub == k) | (lane == first + k), 0.0, rows)
            rows = rest - jnp.concatenate([column] * copies, axis=1) * row
    return rows


def invert(a_ref):
    size = a_ref.shape[0]
    sub = lax.broadcasted_iota(jnp.int32, (size, size), 0) // BLOCK
    lane = lax.broadcasted_iota(jnp.int32, (size, size), 1) // BLOCK
    eye_row = lax.broadcasted_iota(jnp.int32, (BLOCK, size), 0)
    eye_lane = lax.broadcasted_iota(jnp.int32, (BLOCK, size), 1)
    rows = a_ref[0:BLOCK, :]
    for k in range(size // BLOCK):
        first = k * BLOCK
        minus = jnp.where(eye_row + first == eye_lane, -1.0, 0.0)
        panel = jnp.where(eye_lane // BLOCK == k, minus, rows)
        scaled = sweep(rows, first)
        n = first + BLOCK
        if n < size:
            rows = jnp.where(eye_lane // BLOCK == k, 0.0, a_ref[n : n + BLOCK, :])
            rows = rows - dot32(panel[:, n : n + BLOCK], scaled, TN)
        rest = jnp.where((sub == k) | (lane == k), 0.0, a_ref[...])
        a_ref[...] = rest - dot32(panel, scaled, TN)


def mix(gram, factor, a_ref):
    size = factor.shape[0]
    same = lax.broadcasted_iota(jnp.int32, (size, size), 0) == lax.broadcasted_iota(
        jnp.int32, (size, size), 1
    )
    a_ref[...] = jnp.where(same, 1.0, 0.0) + dot32(factor, dot32(gram, factor, NN), TN)
    invert(a_ref)
    return dot32(factor, dot32(-a_ref[...], factor, NT), NN)


def level_two(s_ref, f_ref, next_ref, x_ref, xv_ref, a_ref):
    w = f_ref.shape[0]
    mixer = mix(s_ref[2 * w : 3 * w], f_ref[...], a_ref)
    t20, t21 = s_ref[0:w], s_ref[w : 2 * w]
    x20, x21 = dot32(mixer, t20, NN), dot32(mixer, t21, NN)
    x_ref[0:w] = x20
    x_ref[w : 2 * w] = x21
    vecs = 6 * w
    h0, h1, h2 = [s_ref[vecs + i * VEC : vecs + (i + 1) * VEC] for i in range(3)]
    xv = dot32(h2, mixer, NN)
    xv_ref[...] = xv
    next_ref[0:w] = s_ref[3 * w : 4 * w] - dot32(t21, x20, TN)
    next_ref[w : 2 * w] = s_ref[4 * w : 5 * w] - dot32(t21, x21, TN)
    next_ref[2 * w : 3 * w] = s_ref[5 * w : 6 * w] - dot32(t20, x20, TN)
    next_ref[3 * w : 3 * w + VEC] = h0 - dot32(xv, t20, NN)
    next_ref[3 * w + VEC : 3 * w + 2 * VEC] = h1 - dot32(xv, t21, NN)


def level_one(s_ref, f_ref, x2_ref, x2v_ref, next_ref, x_ref, xv_ref, a_ref):
    w = f_ref.shape[0]
    mixer = mix(s_ref[w : 2 * w], f_ref[...], a_ref)
    t10 = s_ref[0:w]
    x10 = dot32(mixer, t10, NN)
    h0, h1 = [s_ref[3 * w + i * VEC : 3 * w + (i + 1) * VEC] for i in range(2)]
    xv = dot32(h1, mixer, NN)
    next_ref[0:w] = s_ref[2 * w : 3 * w] - dot32(t10, x10, TN)
    next_ref[w : w + VEC] = h0 - dot32(xv, t10, NN)
    next_ref[w + VEC :] = jnp.zeros_like(next_ref[w + VEC :])
    x21 = x2_ref[w : 2 * w]
    x_ref[0:w] = x10
    x_ref[w : 2 * w] = x2_ref[0:w] - dot32(x21, x10, NN)
    xv_ref[0:VEC] = xv
    xv_ref[VEC : 2 * VEC] = x2v_ref[...] - dot32(xv, x21, NT)


def level_zero(s_ref, f_ref, x1_ref, x1v_ref, k_ref, kv_ref, a_ref):
    w = f_ref.shape[0]
    gram = s_ref[0:w]
    mixer = mix(gram, f_ref[...], a_ref)
    x00 = dot32(mixer, gram, NN)
    xv = dot32(s_ref[w : w + VEC], mixer, NN)
    k_ref[0:w] = x00
    kv_ref[0:VEC] = xv
    for i in range(2):
        x = x1_ref[i * w : (i + 1) * w]
        k_ref[(i + 1) * w : (i + 2) * w] = x - dot32(x, x00, NN)
        v = x1v_ref[i * VEC : (i + 1) * VEC]
        kv_ref[(i + 1) * VEC : (i + 2) * VEC] = v - dot32(xv, x, NT)


def level_call(body, name, args, outs):
    w = args[1].shape[0]
    return pl.pallas_call(
        body,
        out_shape=[jax.ShapeDtypeStruct((rows, w), jnp.float32) for rows in outs],
        in_specs=[pl.BlockSpec(memory_space=pltpu.VMEM)] * len(args),
        out_specs=[pl.BlockSpec(memory_space=pltpu.VMEM)] * len(outs),
        scratch_shapes=[pltpu.VMEM((w, w), jnp.float32)],
        compiler_params=pltpu.CompilerParams(vmem_limit_bytes=32 << 20),
        name=name,
    )(*args)


def dot16(a, b, dims):
    return lax.dot_general(a, b, (dims, ((), ())), preferred_element_type=jnp.float32)


def basis_kernel(nodes, order_ref, x_ref, y_ref, *rest):
    marks, out_ref = rest[:3], rest[3]
    tile, rows = order_ref.shape[0], x_ref.shape[0]
    w = marks[0].shape[1]
    place = lax.broadcasted_iota(jnp.int32, (tile, rows), 1)
    same = place == order_ref[...]
    pick = jnp.where(same, 1.0, 0.0).astype(jnp.bfloat16)
    tree = dot16(pick, x_ref[...], NN)
    score = jnp.sum(jnp.where(same, y_ref[...], 0.0), axis=1, keepdims=True)
    row_sq = jnp.sum(tree * tree, axis=1, keepdims=True)
    tree = tree.astype(jnp.bfloat16)
    for level in range(3):
        mark = marks[level][0]
        cross = dot16(tree, mark, NT)
        wide = mark.astype(jnp.float32)
        mark_sq = dot32(jnp.ones((8, wide.shape[1]), jnp.float32), wide * wide, NT)[:1]
        dist_sq = row_sq + mark_sq - 2.0 * cross
        scaled = root_five * jnp.sqrt(dist_sq + 1e-06) / length_scale
        value = (1.0 + scaled + scaled * scaled / 3.0) * jnp.exp(-scaled)
        out_ref[:, level * w : (level + 1) * w] = value.astype(jnp.bfloat16)
    lane = lax.broadcasted_iota(jnp.int32, (tile, PAD), 1)
    out_ref[:, 3 * w :] = jnp.where(lane == 0, score, 0.0).astype(jnp.bfloat16)


def make_basis(nodes, order, features, rhs, landmarks):
    rows, width = features.shape
    w = landmarks.shape[1]
    mark = lambda level: pl.BlockSpec((1, w, width), lambda i, nodes: (nodes[level], 0, 0))
    return pl.pallas_call(
        basis_kernel,
        grid_spec=pltpu.PrefetchScalarGridSpec(
            num_scalar_prefetch=1,
            grid=(rows // TILE,),
            in_specs=[
                pl.BlockSpec((TILE, 1), lambda i, nodes: (i, 0)),
                pl.BlockSpec((rows, width), lambda i, nodes: (0, 0)),
                pl.BlockSpec((1, rows), lambda i, nodes: (0, 0)),
                mark(0),
                mark(1),
                mark(2),
            ],
            out_specs=pl.BlockSpec((TILE, 3 * w + PAD), lambda i, nodes: (i, 0)),
        ),
        out_shape=jax.ShapeDtypeStruct((rows, 3 * w + PAD), jnp.bfloat16),
        compiler_params=pltpu.CompilerParams(vmem_limit_bytes=32 << 20),
        name="make_basis",
    )(nodes, order[:, None], features, rhs.astype(jnp.float32)[None, :], *[landmarks] * 3)


def solve_kernel(g_ref, basis_ref, w_ref, sum_ref):
    i = pl.program_id(0)
    tile = g_ref.shape[0]
    w = sum_ref.shape[1]
    solved = dot16(g_ref[...], basis_ref[...], NN)
    w_ref[...] = solved
    parts = halves(solved)
    mine = basis_ref[pl.ds(pl.multiple_of(i * tile, tile), tile), : 3 * w]

    @pl.when(i == 0)
    def _():
        sum_ref[...] = jnp.zeros_like(sum_ref)

    for slot, (level, q) in enumerate(((2, 0), (2, 1), (2, 2), (1, 0), (1, 1), (0, 0))):
        basis = mine[:, level * w : (level + 1) * w]
        sum_ref[slot * w : (slot + 1) * w] += sum(
            dot16(basis, part[:, q * w : (q + 1) * w], TN) for part in parts
        )
    h = sum(dot16(part[:, 3 * w :], mine, TN) for part in parts)[:VEC]
    for level in range(3):
        at = 6 * w + level * VEC
        sum_ref[at : at + VEC] += h[:, level * w : (level + 1) * w]


def solve_leaf(inverse, basis, w):
    rows, width = basis.shape
    total = 6 * w + 4 * VEC
    return pl.pallas_call(
        solve_kernel,
        grid=(rows // TILE,),
        in_specs=[
            pl.BlockSpec((TILE, rows), lambda i: (i, 0)),
            pl.BlockSpec((rows, width), lambda i: (0, 0)),
        ],
        out_specs=[
            pl.BlockSpec((TILE, width), lambda i: (i, 0)),
            pl.BlockSpec((total, w), lambda i: (0, 0)),
        ],
        out_shape=[
            jax.ShapeDtypeStruct((rows, width), jnp.float32),
            jax.ShapeDtypeStruct((total, w), jnp.float32),
        ],
        compiler_params=pltpu.CompilerParams(vmem_limit_bytes=40 << 20),
        name="solve_leaf",
    )(inverse, basis)


def finish_kernel(w_ref, k_ref, kv_ref, alpha_ref, out_ref):
    w = k_ref.shape[1]
    high, low = halves(w_ref[:, : 3 * w])
    k_high, k_low = halves(k_ref[...])
    change = dot16(high, k_high, NN) + dot16(high, k_low, NN) + dot16(low, k_high, NN)
    out_ref[...] = w_ref[:, :w] - change
    shape = (VEC, PAD)
    first = (lax.broadcasted_iota(jnp.int32, shape, 0) == 0) & (
        lax.broadcasted_iota(jnp.int32, shape, 1) == 0
    )
    kept = jnp.where(first, 1.0, 0.0)
    alpha = dot32(kept, w_ref[:, 3 * w :], NT)
    for level in range(3):
        part = w_ref[:, level * w : (level + 1) * w]
        alpha = alpha - dot32(kv_ref[level * VEC : (level + 1) * VEC], part, NT)
    alpha_ref[...] = alpha


def finish(solved, k, kv):
    rows, width = solved.shape
    w = k.shape[1]
    return pl.pallas_call(
        finish_kernel,
        grid=(rows // TILE,),
        in_specs=[
            pl.BlockSpec((TILE, width), lambda i: (i, 0)),
            pl.BlockSpec(k.shape, lambda i: (0, 0)),
            pl.BlockSpec(kv.shape, lambda i: (0, 0)),
        ],
        out_specs=[
            pl.BlockSpec((VEC, TILE), lambda i: (0, i)),
            pl.BlockSpec((TILE, w), lambda i: (i, 0)),
        ],
        out_shape=[
            jax.ShapeDtypeStruct((VEC, rows), jnp.float32),
            jax.ShapeDtypeStruct((rows, w), jnp.float32),
        ],
        compiler_params=pltpu.CompilerParams(vmem_limit_bytes=32 << 20),
        name="finish",
    )(solved, k, kv)


def per_device(features, rhs, leaf_order, leaf_inverse, landmarks, core_factor):
    leaf = lax.axis_index("leaf")
    digits = lax.axis_size("leaf").bit_length() - 1
    w = core_factor.shape[1]
    nodes = [2**level - 1 + jnp.right_shift(leaf, digits - level) for level in range(3)]
    factors = [lax.dynamic_index_in_dim(core_factor, n, 0, keepdims=False) for n in nodes]
    basis = make_basis(
        jnp.stack(nodes).astype(jnp.int32), leaf_order, features, rhs, landmarks
    )
    solved, buf = solve_leaf(leaf_inverse, basis, w)
    buf = node_sum(buf, tuple(range(1, digits - 2)), True, 0)
    buf, x2, x2v = level_call(
        level_two, "level_two", (buf, factors[2]), (3 * w + 2 * VEC, 2 * w, VEC)
    )
    buf = node_sum(buf, (digits - 2,), False, 1)
    buf, x1, x1v = level_call(
        level_one, "level_one", (buf, factors[1], x2, x2v), (w + 2 * VEC, 2 * w, 2 * VEC)
    )
    buf = node_sum(buf, (digits - 1,), False, 2)
    k, kv = level_call(level_zero, "level_zero", (buf, factors[0], x1, x1v), (3 * w, 3 * VEC))
    alpha, out = finish(solved, k, kv)
    return (alpha[0], out)


def solution(mesh):
    in_specs = (
        P(("parts", "leaf"), None),
        P(("parts", "leaf")),
        P(("parts", "leaf")),
        P(("parts", "leaf"), None),
        P("parts", None, None),
        P("parts", None, None),
    )
    out_specs = (P(("parts", "leaf")), P(("parts", "leaf"), None))
    return jax.shard_map(
        per_device, mesh=mesh, in_specs=in_specs, out_specs=out_specs, check_vma=False
    )
```
